32 devices in a mesh: gx: 8 (over z, x), gy: 4 (over y, core).
Axes of the slice: x: 2, y: 2, z: 4, core: 2. Of those that a mesh axis runs over, the one named last changes fastest.
Arguments:
- hidden_in: bfloat16 [16, 5120], P(None, 'gx'), may hold values from -60 to 60
- norm1_gain: float32 [5120], P('gx'), may hold values from 0.1 to 1.9
- norm1_bias: float32 [5120], P('gx'), may hold values from -4 to 4
- norm2_gain: float32 [5120], P('gx'), may hold values from 0.1 to 1.9
- norm2_bias: float32 [5120], P('gx'), may hold values from -4 to 4
- w_qkv: bfloat16 [5120, 15360], P('gx', 'gy'), may hold values from -0.078125 to 0.078125
- b_qkv: float32 [15360], P('gy'), may hold values from -4 to 4
- w_out: bfloat16 [5120, 5120], P('gy', 'gx'), may hold values from -0.078125 to 0.078125
- b_out: float32 [5120], P('gx'), may hold values from -4 to 4
- w_up: bfloat16 [5120, 20480], P('gx', 'gy'), may hold values from -0.078125 to 0.078125
- b_up: float32 [20480], P('gy'), may hold values from -4 to 4
- w_down: bfloat16 [20480, 5120], P('gy', 'gx'), may hold values from -0.0390625 to 0.0390625
- b_down: float32 [5120], P('gx'), may hold values from -4 to 4
- key_cache: bfloat16 [16, 40, 1024, 128], P('gx', 'gy'), may hold values from -70 to 70
- value_cache: bfloat16 [16, 40, 1024, 128], P('gx', 'gy'), may hold values from -6 to 6
- lengths: int32 [16], replicated, may hold values from 1 to 1024, 8192 in all
- assignment: int32 [16], replicated, may hold values from 0 to 15, each once
Outputs:
- hidden_out: bfloat16 [16, 5120], P(None, 'gx')
- new_keys: bfloat16 [16, 40, 1024, 128], P('gx', 'gy')
- new_values: bfloat16 [16, 40, 1024, 128], P('gx', 'gy')
The draws below stay inside these ranges and needn't reach their ends.
Inputs may be any that keep to these rules, and one draw needn't show every extreme that they name: `lengths`: each request's length, the largest exactly 1024. `assignment`: a permutation: every slot holds exactly one request.
All inputs are finite; a program needn't handle non-finite values.
Results may differ from the reference program's by a relative error of at most 0.0068.
Values may be sent and summed in bfloat16 or wider, within the bound.
A program may use at most 128 MiB of HBM per device.

```python
import math
import jax
import jax.numpy as jnp
import numpy as np
from jax import lax

D = 5120
HEADS = 40
HD = 128
FF = 20480
ROT = 32
MAXLEN = 1024
REQUESTS = 16


def draw_hidden_in(key, part):
    first_key = jax.random.fold_in(jax.random.fold_in(key, 11), 0)
    ramp = 0.5 + 1.5 * jnp.arange(D, dtype=jnp.float32) / D
    base = jnp.clip(jax.random.normal(first_key, (REQUESTS, D), jnp.float32), -6.0, 6.0)
    return (base * ramp).astype(jnp.bfloat16)


def draw_key_cache(key, part):
    first_key = jax.random.fold_in(jax.random.fold_in(key, 23), 0)
    shape = (REQUESTS, HEADS, MAXLEN, HD)
    base = jnp.clip(jax.random.normal(first_key, shape, jnp.float32), -6.0, 6.0)
    return base.astype(jnp.bfloat16)


def block_levels(key, extent, shards, low, top_value):
    def one(dim, blocks):
        heights = jax.random.uniform(jax.random.fold_in(jax.random.fold_in(key, 6), dim), (blocks,), jnp.float32, low / len(shards), top_value / len(shards))
        return jnp.repeat(jnp.exp(heights), extent[dim] // blocks).reshape((-1,) + (1,) * (len(extent) - dim - 1))

    factor_of = one(*shards[0])
    for cut in shards[1:]:
        factor_of = factor_of * one(*cut)
    return factor_of


def split_up(amount, total, most, slope):
    weights = [(1 << 20) // math.isqrt(rank ** slope) + 1 for rank in range(2, amount + 1)]
    rest, counts = total - most - (amount - 1), [1] * (amount - 1)
    while rest > 0:
        free = [i for i in range(amount - 1) if counts[i] < most]
        mass, remaining = sum([weights[i] for i in free]), rest
        for i in free:
            extra = min(most - counts[i], max(1, remaining * weights[i] // mass), rest)
            counts[i] = counts[i] + extra
            rest = rest - extra
    return np.array([most] + counts)


def ragged(key, count, total, limit, slope):
    if count == 2:
        one = jax.random.randint(key, (), max(1, total - limit), min(limit, total - 1) + 1)
        return jnp.stack([one, total - one])
    sizes = jnp.asarray(split_up(count, total, limit, slope), jnp.int32)
    pairs = (count - 1) // 2
    giver, taker = sizes[1:1 + 2 * pairs:2], sizes[2:2 + 2 * pairs:2]
    margin = jnp.minimum(giver - 1, limit - taker)
    shifted = jax.random.randint(jax.random.fold_in(key, 1), (pairs,), 0, 1 << 20) % (margin + 1)
    sizes = sizes.at[1:1 + 2 * pairs:2].set(giver - shifted).at[2:2 + 2 * pairs:2].set(taker + shifted)
    return sizes[jax.random.permutation(jax.random.fold_in(key, 2), count)]


def gaussian(own_key, extent, width, most, shards=(), kind=jnp.bfloat16):
    drawn = width * jax.random.normal(own_key, extent, jnp.float32)
    if shards:
        drawn = drawn * block_levels(own_key, extent, shards, -0.22, 0.18)
    return jnp.clip(drawn, -most, most).astype(kind)


def setup_inputs(seed: int = 0) -> dict:
    streams_of = jax.random.split(jax.random.key(seed), 18)
    hidden_in = draw_hidden_in(jax.random.fold_in(streams_of[17], 71), 0)
    norm1_gain = jnp.clip(1.0 + 0.18 * jax.random.normal(streams_of[1], (D,), jnp.float32), 0.1, 1.9)
    norm1_bias = gaussian(streams_of[2], (D,), 0.3, 4.0, ((0, 8),), jnp.float32)
    norm2_gain = jnp.clip(1.0 + 0.18 * jax.random.normal(streams_of[3], (D,), jnp.float32), 0.1, 1.9)
    norm2_bias = gaussian(streams_of[4], (D,), 0.3, 4.0, ((0, 8),), jnp.float32)
    w_qkv = gaussian(streams_of[5], (D, 3 * D), D ** -0.5, 0.078125, ((0, 8), (1, 4)))
    b_qkv = gaussian(streams_of[6], (3 * D,), 0.5, 4.0, ((0, 4),), jnp.float32)
    w_out = gaussian(streams_of[7], (D, D), D ** -0.5, 0.078125, ((0, 4), (1, 8)))
    b_out = gaussian(streams_of[8], (D,), 0.5, 4.0, ((0, 8),), jnp.float32)
    w_up = gaussian(streams_of[9], (D, FF), D ** -0.5, 0.078125, ((0, 8), (1, 4)))
    b_up = gaussian(streams_of[10], (FF,), 0.5, 4.0, ((0, 4),), jnp.float32)
    w_down = gaussian(streams_of[11], (FF, D), FF ** -0.5, 0.0390625, ((0, 4), (1, 8)))
    b_down = gaussian(streams_of[12], (D,), 0.5, 4.0, ((0, 8),), jnp.float32)
    key_cache = draw_key_cache(jax.random.fold_in(streams_of[17], 71), 0)
    value_cache = gaussian(streams_of[14], (REQUESTS, HEADS, MAXLEN, HD), 1.0, 6.0, ((0, 8), (1, 4)))
    lengths = ragged(streams_of[15], REQUESTS, REQUESTS * MAXLEN // 2, MAXLEN, 2).astype(jnp.int32)
    assignment = jax.random.permutation(streams_of[16], REQUESTS).astype(jnp.int32)
    return {"hidden_in": hidden_in, "norm1_gain": norm1_gain, "norm1_bias": norm1_bias, "norm2_gain": norm2_gain, "norm2_bias": norm2_bias, "w_qkv": w_qkv, "b_qkv": b_qkv, "w_out": w_out, "b_out": b_out, "w_up": w_up, "b_up": b_up, "w_down": w_down, "b_down": b_down, "key_cache": key_cache, "value_cache": value_cache, "lengths": lengths, "assignment": assignment}


def rotate(tensor, position):
    half_rot = ROT // 2
    frequency = 10000.0 ** (-2.0 * jnp.arange(half_rot, dtype=jnp.float32) / ROT)
    angle = position.astype(jnp.float32)[:, None, None] * frequency
    cosine = jnp.cos(angle)
    sine = jnp.sin(angle)
    first_half = tensor[..., :half_rot]
    second_half = tensor[..., half_rot:ROT]
    return jnp.concatenate([first_half * cosine - second_half * sine, second_half * cosine + first_half * sine, tensor[..., ROT:]], axis=-1)

def reference(hidden_in, norm1_gain, norm1_bias, norm2_gain, norm2_bias, w_qkv, b_qkv, w_out, b_out, w_up, b_up, w_down, b_down, key_cache, value_cache, lengths, assignment):
    wide_in = hidden_in.astype(jnp.float32)
    row_mean = lax.optimization_barrier(jnp.sum(wide_in, axis=1)) / D
    row_var = lax.optimization_barrier(jnp.sum(wide_in * wide_in, axis=1)) / D - row_mean * row_mean
    normed = (wide_in - row_mean[:, None]) * lax.rsqrt(row_var + 1e-05)[:, None]
    attn_in = (normed * norm1_gain + norm1_bias).astype(jnp.bfloat16)
    mlp_in = (normed * norm2_gain + norm2_bias).astype(jnp.bfloat16)
    qkv = jnp.dot(attn_in, w_qkv, preferred_element_type=jnp.float32) + b_qkv
    qkv = qkv.reshape(REQUESTS, HEADS, 3, HD)
    position = lengths - 1
    query = rotate(qkv[:, :, 0], position).astype(jnp.bfloat16)
    new_key = rotate(qkv[:, :, 1], position).astype(jnp.bfloat16)
    new_value = qkv[:, :, 2].astype(jnp.bfloat16)
    new_keys = key_cache.at[assignment, :, position, :].set(new_key)
    new_values = value_cache.at[assignment, :, position, :].set(new_value)
    scale = HD ** (-0.5)

    def attend_one(items):
        query_row, slot_id, length = items
        keys = lax.dynamic_index_in_dim(new_keys, slot_id, 0, keepdims=False).astype(jnp.float32)
        values = lax.dynamic_index_in_dim(new_values, slot_id, 0, keepdims=False).astype(jnp.float32)
        scores = jnp.einsum('hd,hpd->hp', query_row.astype(jnp.float32), keys) * scale
        valid = jnp.arange(MAXLEN, dtype=jnp.int32)[None, :] < length
        scores = jnp.where(valid, scores, -1e+30)
        top_score = lax.optimization_barrier(jnp.max(scores, axis=1))
        weights = jnp.where(valid, jnp.exp(scores - top_score[:, None]), 0.0)
        total = lax.optimization_barrier(jnp.sum(weights, axis=1))
        weights_low = lax.optimization_barrier(weights.astype(jnp.bfloat16))
        weighted = jnp.einsum('hp,hpd->hd', weights_low.astype(jnp.float32), values)
        return (weighted / total[:, None]).astype(jnp.bfloat16)
    attended = lax.map(attend_one, (query, assignment, lengths)).reshape(REQUESTS, D)
    attn_part = jnp.dot(attended, w_out, preferred_element_type=jnp.float32)
    up = jnp.dot(mlp_in, w_up, preferred_element_type=jnp.float32) + b_up
    hidden = jax.nn.gelu(up, approximate=False).astype(jnp.bfloat16)
    mlp_part = jnp.dot(hidden, w_down, preferred_element_type=jnp.float32)
    hidden_out = (wide_in + attn_part + mlp_part + b_out + b_down).astype(jnp.bfloat16)
    return (hidden_out, new_keys, new_values)
```

```python
import functools

import jax
import jax.numpy as jnp
import numpy as np
from jax import lax
from jax.experimental import pallas as pl
from jax.experimental.pallas import tpu as pltpu
from jax.sharding import PartitionSpec as P

HD = 128
ROT = 32
F32 = jnp.float32
BF16 = jnp.bfloat16
MESH = pl.DeviceIdType.MESH
ANY = pl.BlockSpec(memory_space=pl.ANY)
VMEM = pl.BlockSpec(memory_space=pltpu.VMEM)
SMEM = pl.BlockSpec(memory_space=pltpu.SMEM)


def slot_rows(asg_ref):
    requests = asg_ref.shape[1]
    slots = lax.broadcasted_iota(jnp.int32, (requests, requests), 0)
    return jnp.where(slots == asg_ref[...], 1.0, 0.0).astype(BF16)


def send(src, dst, ssem, rsem, where):
    copy = pltpu.make_async_remote_copy(
        src_ref=src, dst_ref=dst, send_sem=ssem, recv_sem=rsem,
        device_id=where, device_id_type=MESH,
    )
    copy.start()
    return copy


def project_kernel(
    n, m, h_ref, g1_ref, b1_ref, g2_ref, b2_ref, asg_ref, bq_ref, bu_ref, wq_hbm, wu_hbm,
    qkv_ref, hid_ref,
    wq, wu, st_own, st_in, q_send, q_in, u_part, u_send, u_in,
    wsem, s_ssem, s_rsem, q_ssem, q_rsem, u_ssem, u_rsem,
):
    me = lax.axis_index("gx")
    rg_count = n // m
    requests, depth = h_ref.shape
    rows = q_send.shape[1]
    u_rows, u_cols = u_send.shape[1:]
    my_col, my_group = lax.rem(me, m), me // m
    load_q = pltpu.make_async_copy(wq_hbm, wq, wsem.at[m])
    load_q.start()
    order = list(range(1, m)) + [0]
    loads = {}
    for k in order:
        col = lax.rem(my_col + k, m)
        loads[k] = pltpu.make_async_copy(
            wu_hbm.at[:, pl.ds(pl.multiple_of(col * u_cols, 128), u_cols)], wu.at[k], wsem.at[k]
        )
        loads[k].start()
    barrier = pltpu.get_barrier_semaphore()
    for k in range(1, n):
        pl.semaphore_signal(barrier, inc=1, device_id={"gx": lax.rem(me + k, n)}, device_id_type=MESH)

    place = slot_rows(asg_ref)
    x = jnp.dot(place, h_ref[...], preferred_element_type=F32)
    sums = jnp.sum(x, axis=1, keepdims=True)
    squares = jnp.sum(x * x, axis=1, keepdims=True)
    lane = lax.broadcasted_iota(jnp.int32, (requests, 128), 1)
    st_own[...] = jnp.where(lane == 0, sums, jnp.where(lane == 1, squares, 0.0))
    pl.semaphore_wait(barrier, n - 1)
    stats = [
        send(st_own, st_in.at[k], s_ssem.at[k], s_rsem.at[k], {"gx": lax.rem(me + k, n)})
        for k in range(1, n)
    ]
    total = st_own[...]
    for k in range(1, n):
        stats[k - 1].wait_recv()
        total = total + st_in[k]
    width = depth * n
    mean = total[:, 0:1] / width
    var = total[:, 1:2] / width - mean * mean
    normed = (x - mean) * lax.rsqrt(var + 1e-05)
    attn_in = (normed * g1_ref[...] + b1_ref[...]).astype(BF16)
    mlp_in = (normed * g2_ref[...] + b2_ref[...]).astype(BF16)

    load_q.wait()
    qkv = jnp.dot(attn_in, wq[...], preferred_element_type=F32)
    for p in range(n):
        q_send[p] = qkv[p * rows : (p + 1) * rows, :]
    q_copies = []
    for k in range(1, n):
        peer = lax.rem(me + k, n)
        q_copies.append(send(q_send.at[peer], q_in.at[k], q_ssem.at[k], q_rsem.at[k], {"gx": peer}))
    u_copies = []
    for k in order:
        loads[k].wait()
        part = jnp.dot(mlp_in, wu[k], preferred_element_type=F32)
        if rg_count > 1:
            u_part[...] = part
        for j in list(range(1, rg_count)) + [0]:
            group = lax.rem(my_group + j, rg_count)
            peer = group * m + lax.rem(my_col + k, m)
            at = j * m + k
            if rg_count > 1:
                own = u_part[pl.ds(pl.multiple_of(group * u_rows, u_rows), u_rows), :]
            else:
                own = part
            u_send[at] = own.astype(BF16)
            if at:
                u_copies.append(send(u_send.at[at], u_in.at[at], u_ssem.at[at], u_rsem.at[at], {"gx": peer}))
    total_q = q_send[me] + bq_ref[...]
    for k in range(1, n):
        q_copies[k - 1].wait_recv()
        total_q = total_q + q_in[k]
    qkv_ref[...] = total_q
    for copy in u_copies:
        copy.wait_recv()
    up = own.astype(F32) + bu_ref[my_col]
    for at in range(1, n):
        up = up + u_in[at].astype(F32)
    hid_ref[...] = (0.5 * up * (1.0 + lax.erf(up * np.float32(0.5**0.5)))).astype(BF16)
    for copy in stats + q_copies + u_copies:
        copy.wait_send()


def attend_kernel(
    len_ref, asg_ref, qkv_ref, freq_ref, k_hbm, v_hbm,
    att_ref, nk_hbm, nv_hbm,
    kbuf, vbuf, q_scr, k_scr, v_scr, sc, o_scr, isem, osem,
):
    rows, heads, span, _ = kbuf.shape
    requests = len_ref.shape[0]
    first = lax.axis_index("gx") * rows
    loads = []
    for s in range(rows):
        for i, (hbm, buf) in enumerate(((k_hbm, kbuf), (v_hbm, vbuf))):
            copy = pltpu.make_async_copy(hbm.at[s], buf.at[s], isem.at[2 * s + i])
            copy.start()
            loads.append(copy)
    lane = lax.broadcasted_iota(jnp.int32, (1, HD), 1)
    half = ROT // 2
    places = lax.broadcasted_iota(jnp.int32, (heads, span), 1)
    stores = []
    for s in range(rows):
        def find(r, value):
            return jnp.where(asg_ref[r] == first + s, len_ref[r], value)
        length = lax.fori_loop(0, requests, find, jnp.int32(1))
        position = length - 1
        angle = position.astype(F32) * freq_ref[...]
        cosine, sine = jnp.cos(angle), jnp.sin(angle)
        c = jnp.where(lane < ROT, cosine, 1.0)
        s1 = jnp.where(lane < half, -sine, 0.0)
        s2 = jnp.where((lane >= half) & (lane < ROT), sine, 0.0)

        def turn(t):
            return t * c + pltpu.roll(t, HD - half, 1) * s1 + pltpu.roll(t, half, 1) * s2

        for h in range(heads):
            q_scr[h : h + 1, :] = qkv_ref[s : s + 1, (3 * h) * HD : (3 * h + 1) * HD]
            k_scr[h : h + 1, :] = qkv_ref[s : s + 1, (3 * h + 1) * HD : (3 * h + 2) * HD]
            v_scr[h : h + 1, :] = qkv_ref[s : s + 1, (3 * h + 2) * HD : (3 * h + 3) * HD]
        query = turn(q_scr[...]).astype(BF16)
        new_key = turn(k_scr[...])
        new_value = v_scr[...]
        base = pl.multiple_of((position // 16) * 16, 16)
        hit = lax.broadcasted_iota(jnp.int32, (16, HD), 0) == position - base
        for i, (buf, hbm, fresh) in enumerate(((kbuf, nk_hbm, new_key), (vbuf, nv_hbm, new_value))):
            loads[2 * s + i].wait()
            for h in range(heads):
                old = buf[s, h, pl.ds(base, 16), :].astype(F32)
                buf[s, h, pl.ds(base, 16), :] = jnp.where(hit, fresh[h : h + 1, :], old).astype(BF16)
            copy = pltpu.make_async_copy(buf.at[s], hbm.at[s], osem.at[2 * s + i])
            copy.start()
            stores.append(copy)
            if i == 0:
                for h in range(heads):
                    sc[h : h + 1, :] = lax.dot_general(
                        query[h : h + 1, :], kbuf[s, h], (((1,), (1,)), ((), ())),
                        preferred_element_type=F32,
                    )
                scores = sc[0:heads, :] * np.float32(HD**-0.5)
                valid = places < length
                scores = jnp.where(valid, scores, -1e30)
                top = jnp.max(scores, axis=1, keepdims=True)
                weights = jnp.where(valid, jnp.exp(scores - top), 0.0)
                total = jnp.sum(weights, axis=1, keepdims=True)
                low = weights.astype(BF16)
        for h in range(heads):
            o_scr[h : h + 1, :] = jnp.dot(low[h : h + 1, :], vbuf[s, h], preferred_element_type=F32)
        out = (o_scr[0:heads, :] / total).astype(BF16).astype(F32)
        for h in range(heads):
            att_ref[s : s + 1, h * HD : (h + 1) * HD] = out[h : h + 1, :]
    for copy in stores:
        copy.wait()


def output_kernel(
    n, m, ny, att_ref, hid_ref, h_ref, asg_ref, bo_ref, bd_ref, wo_hbm, wd_hbm,
    out_ref,
    wo, wd, h_all, a_all, a_rows, y_send, y_in,
    wsem, h_ssem, h_rsem, a_ssem, a_rsem, y_ssem, y_rsem,
):
    me, my = lax.axis_index("gx"), lax.axis_index("gy")
    rows = att_ref.shape[0]
    cols = hid_ref.shape[1]
    load_d = pltpu.make_async_copy(wd_hbm, wd, wsem.at[0])
    load_o = pltpu.make_async_copy(wo_hbm, wo, wsem.at[1])
    load_d.start()
    load_o.start()
    barrier = pltpu.get_barrier_semaphore()
    for k in range(1, n):
        pl.semaphore_signal(barrier, inc=1, device_id={"gx": lax.rem(me + k, n)}, device_id_type=MESH)
    for k in range(1, ny):
        pl.semaphore_signal(barrier, inc=1, device_id={"gy": lax.rem(my + k, ny)}, device_id_type=MESH)
    h_all[me] = hid_ref[...]
    a_all[me] = att_ref[...]
    pl.semaphore_wait(barrier, n + ny - 2)
    a_copies, h_copies = [], []
    for k in range(1, n):
        peer = {"gx": lax.rem(me + k, n)}
        h_copies.append(send(h_all.at[me], h_all.at[me], h_ssem.at[k], h_rsem.at[k], peer))
    for k in range(1, n):
        peer = {"gx": lax.rem(me + k, n)}
        a_copies.append(send(a_all.at[me], a_all.at[me], a_ssem.at[k], a_rsem.at[k], peer))
    place = slot_rows(asg_ref)
    x = jnp.dot(place, h_ref[...], preferred_element_type=F32) + bo_ref[...] + bd_ref[...]
    for copy in h_copies:
        copy.wait_recv()
    load_d.wait()
    acc = jnp.zeros(y_send.shape, F32)
    for c in range(m):
        parts = [h_all[g * m + c] for g in range(n // m)]
        block = parts[0] if len(parts) == 1 else jnp.concatenate(parts, axis=0)
        acc = acc + jnp.dot(block, wd[c * cols : (c + 1) * cols, :], preferred_element_type=F32)
    for copy in a_copies:
        copy.wait_recv()
    for p in range(n):
        a_rows[p * rows : (p + 1) * rows, :] = a_all[p]
    load_o.wait()
    acc = acc + jnp.dot(a_rows[...].astype(BF16), wo[...], preferred_element_type=F32)
    y_send[...] = acc
    y_copies = []
    for k in range(1, ny):
        peer = {"gy": lax.rem(my + k, ny)}
        y_copies.append(send(y_send, y_in.at[k], y_ssem.at[k], y_rsem.at[k], peer))
    acc = acc + x
    for k in range(1, ny):
        y_copies[k - 1].wait_recv()
        acc = acc + y_in[k]
    out_ref[...] = lax.dot_general(
        place, acc.astype(BF16), (((0,), (0,)), ((), ())), preferred_element_type=F32
    ).astype(BF16)
    for copy in h_copies + a_copies + y_copies:
        copy.wait_send()


def on_device(
    n, ny, hidden_in, norm1_gain, norm1_bias, norm2_gain, norm2_bias, w_qkv, b_qkv, w_out, b_out,
    w_up, b_up, w_down, b_down, key_cache, value_cache, lengths, assignment,
):
    requests, depth = hidden_in.shape
    rows, heads, span, _ = key_cache.shape
    q_cols = w_qkv.shape[1]
    units = w_up.shape[1]
    m = max(c for c in range(1, n + 1) if n % c == 0 and units % c == 0 and (units // c) % 128 == 0)
    u_rows, u_cols = requests // (n // m), units // m
    asg = assignment.reshape(1, requests)
    dma = pltpu.SemaphoreType.DMA
    row = lambda a: a.reshape(1, a.shape[0])

    qkv, hid = pl.pallas_call(
        functools.partial(project_kernel, n, m),
        out_shape=(
            jax.ShapeDtypeStruct((rows, q_cols), F32),
            jax.ShapeDtypeStruct((u_rows, u_cols), BF16),
        ),
        in_specs=[VMEM] * 8 + [ANY] * 2,
        out_specs=(VMEM, VMEM),
        scratch_shapes=[
            pltpu.VMEM((depth, q_cols), BF16),
            pltpu.VMEM((m, depth, u_cols), BF16),
            pltpu.VMEM((requests, 128), F32),
            pltpu.VMEM((n, requests, 128), F32),
            pltpu.VMEM((n, rows, q_cols), F32),
            pltpu.VMEM((n, rows, q_cols), F32),
            pltpu.VMEM((requests, u_cols), F32),
            pltpu.VMEM((n, u_rows, u_cols), BF16),
            pltpu.VMEM((n, u_rows, u_cols), BF16),
            dma((m + 1,)),
            dma((n,)), dma((n,)), dma((n,)), dma((n,)), dma((n,)), dma((n,)),
        ],
        compiler_params=pltpu.CompilerParams(
            collective_id=0, has_side_effects=True, vmem_limit_bytes=24 << 20
        ),
        name="project",
    )(
        hidden_in, row(norm1_gain), row(norm1_bias), row(norm2_gain), row(norm2_bias), asg,
        row(b_qkv), b_up.reshape(m, 1, u_cols), w_qkv, w_up,
    )

    freq = np.zeros((1, HD), np.float32)
    freq[0, :ROT] = np.tile(10000.0 ** (-2.0 * np.arange(ROT // 2) / ROT), 2)
    padded = -(-heads // 8) * 8
    att, new_keys, new_values = pl.pallas_call(
        attend_kernel,
        out_shape=(
            jax.ShapeDtypeStruct((rows, heads * HD), F32),
            jax.ShapeDtypeStruct(key_cache.shape, BF16),
            jax.ShapeDtypeStruct(value_cache.shape, BF16),
        ),
        in_specs=[SMEM, SMEM, VMEM, VMEM, ANY, ANY],
        out_specs=(VMEM, ANY, ANY),
        scratch_shapes=[
            pltpu.VMEM((rows, heads, span, HD), BF16),
            pltpu.VMEM((rows, heads, span, HD), BF16),
            pltpu.VMEM((padded, HD), F32),
            pltpu.VMEM((padded, HD), F32),
            pltpu.VMEM((padded, HD), F32),
            pltpu.VMEM((padded, span), F32),
            pltpu.VMEM((padded, HD), F32),
            dma((2 * rows,)),
            dma((2 * rows,)),
        ],
        compiler_params=pltpu.CompilerParams(vmem_limit_bytes=20 << 20),
        name="attend",
    )(lengths, assignment, qkv, jnp.asarray(freq), key_cache, value_cache)

    hidden_out = pl.pallas_call(
        functools.partial(output_kernel, n, m, ny),
        out_shape=jax.ShapeDtypeStruct((requests, depth), BF16),
        in_specs=[VMEM] * 6 + [ANY] * 2,
        out_specs=VMEM,
        scratch_shapes=[
            pltpu.VMEM(w_out.shape, BF16),
            pltpu.VMEM(w_down.shape, BF16),
            pltpu.VMEM((n, u_rows, u_cols), BF16),
            pltpu.VMEM((n, rows, heads * HD), F32),
            pltpu.VMEM((requests, heads * HD), F32),
            pltpu.VMEM((requests, depth), F32),
            pltpu.VMEM((ny, requests, depth), F32),
            dma((2,)),
            dma((n,)), dma((n,)), dma((n,)), dma((n,)), dma((ny,)), dma((ny,)),
        ],
        compiler_params=pltpu.CompilerParams(
            collective_id=1, has_side_effects=True, vmem_limit_bytes=20 << 20
        ),
        name="output",
    )(att, hid, hidden_in, asg, row(b_out), row(b_down), w_out, w_down)
    return (hidden_out, new_keys, new_values)


def solution(mesh):
    return jax.shard_map(
        functools.partial(on_device, mesh.shape["gx"], mesh.shape["gy"]),
        mesh=mesh,
        in_specs=(
            P(None, "gx"), P("gx"), P("gx"), P("gx"), P("gx"),
            P("gx", "gy"), P("gy"), P("gy", "gx"), P("gx"),
            P("gx", "gy"), P("gy"), P("gy", "gx"), P("gx"),
            P("gx", "gy", None, None), P("gx", "gy", None, None), P(), P(),
        ),
        out_specs=(P(None, "gx"), P("gx", "gy", None, None), P("gx", "gy", None, None)),
        check_vma=False,
    )
```

```python
import functools

import jax
import jax.numpy as jnp
import numpy as np
from jax import lax
from jax.experimental import pallas as pl
from jax.experimental.pallas import tpu as pltpu
from jax.sharding import PartitionSpec as P

HD = 128
ROT = 32
F32 = jnp.float32
BF16 = jnp.bfloat16
MESH = pl.DeviceIdType.MESH
ANY = pl.BlockSpec(memory_space=pl.ANY)
VMEM = pl.BlockSpec(memory_space=pltpu.VMEM)
SMEM = pl.BlockSpec(memory_space=pltpu.SMEM)
HBM = pl.BlockSpec(memory_space=pltpu.HBM)


def slot_rows(asg_ref):
    requests = asg_ref.shape[1]
    slots = lax.broadcasted_iota(jnp.int32, (requests, requests), 0)
    return jnp.where(slots == asg_ref[...], 1.0, 0.0).astype(BF16)


def send(src, dst, ssem, rsem, where):
    copy = pltpu.make_async_remote_copy(
        src_ref=src, dst_ref=dst, send_sem=ssem, recv_sem=rsem,
        device_id=where, device_id_type=MESH,
    )
    copy.start()
    return copy


def project_kernel(
    n, m, h_ref, g1_ref, b1_ref, g2_ref, b2_ref, asg_ref, bu_ref, wq_hbm, wu_hbm,
    qkv_ref, hid_ref,
    wq, wu, st_own, st_in, q_wide, q_send, q_in, u_part, u_send, u_in,
    wsem, s_ssem, s_rsem, q_ssem, q_rsem, u_ssem, u_rsem,
):
    me = lax.axis_index("gx")
    rg_count = n // m
    requests, depth = h_ref.shape
    rows = requests // n
    tiles = wq.shape[1] // HD
    u_rows, u_cols = u_send.shape[1:]
    my_col, my_group = lax.rem(me, m), me // m
    load_q = pltpu.make_async_copy(wq_hbm, wq, wsem.at[m])
    load_q.start()
    order = list(range(1, m)) + [0]
    loads = {}
    for k in order:
        col = lax.rem(my_col + k, m)
        loads[k] = pltpu.make_async_copy(
            wu_hbm.at[:, pl.ds(pl.multiple_of(col * u_cols, 128), u_cols)], wu.at[k], wsem.at[k]
        )
        loads[k].start()
    barrier = pltpu.get_barrier_semaphore()
    for k in range(1, n):
        pl.semaphore_signal(barrier, inc=1, device_id={"gx": lax.rem(me + k, n)}, device_id_type=MESH)

    place = slot_rows(asg_ref)
    x = jnp.dot(place, h_ref[...], preferred_element_type=F32)
    sums = jnp.sum(x, axis=1, keepdims=True)
    squares = jnp.sum(x * x, axis=1, keepdims=True)
    lane = lax.broadcasted_iota(jnp.int32, (requests, 128), 1)
    st_own[...] = jnp.where(lane == 0, sums, jnp.where(lane == 1, squares, 0.0))
    pl.semaphore_wait(barrier, n - 1)
    stats = [
        send(st_own, st_in.at[k], s_ssem.at[k], s_rsem.at[k], {"gx": lax.rem(me + k, n)})
        for k in range(1, n)
    ]
    total = st_own[...]
    for k in range(1, n):
        stats[k - 1].wait_recv()
        total = total + st_in[k]
    width = depth * n
    mean = total[:, 0:1] / width
    var = total[:, 1:2] / width - mean * mean
    normed = (x - mean) * lax.rsqrt(var + 1e-05)
    attn_in = (normed * g1_ref[...].reshape(1, depth) + b1_ref[...].reshape(1, depth)).astype(BF16)
    mlp_in = (normed * g2_ref[...].reshape(1, depth) + b2_ref[...].reshape(1, depth)).astype(BF16)

    load_q.wait()
    qkv = jnp.dot(attn_in, wq[...], preferred_element_type=F32)
    for p in range(n):
        for j in range(tiles):
            q_wide[p, j * rows : (j + 1) * rows, :] = qkv[
                p * rows : (p + 1) * rows, j * HD : (j + 1) * HD
            ]
    q_send[...] = q_wide[...].astype(BF16)
    q_copies = []
    for k in range(1, n):
        peer = lax.rem(me + k, n)
        q_copies.append(send(q_send.at[peer], q_in.at[k], q_ssem.at[k], q_rsem.at[k], {"gx": peer}))
    u_copies = []
    for k in order:
        loads[k].wait()
        part = jnp.dot(mlp_in, wu[k], preferred_element_type=F32)
        if rg_count > 1:
            u_part[...] = part
        for j in list(range(1, rg_count)) + [0]:
            group = lax.rem(my_group + j, rg_count)
            peer = group * m + lax.rem(my_col + k, m)
            at = j * m + k
            if rg_count > 1:
                own = u_part[pl.ds(pl.multiple_of(group * u_rows, u_rows), u_rows), :]
            else:
                own = part
            u_send[at] = own.astype(BF16)
            if at:
                u_copies.append(send(u_send.at[at], u_in.at[at], u_ssem.at[at], u_rsem.at[at], {"gx": peer}))
    total_q = q_wide[me]
    for k in range(1, n):
        q_copies[k - 1].wait_recv()
        total_q = total_q + q_in[k].astype(F32)
    qkv_ref[...] = total_q
    for copy in u_copies:
        copy.wait_recv()
    up = own.astype(F32) + bu_ref[my_col]
    for at in range(1, n):
        up = up + u_in[at].astype(F32)
    hid_ref[...] = (0.5 * up * (1.0 + lax.erf(up * np.float32(0.5**0.5)))).astype(BF16)
    for copy in stats + q_copies + u_copies:
        copy.wait_send()


def attend_kernel(
    len_ref, asg_ref, qkv_ref, bq_ref, freq_ref, kbuf, vbuf,
    att_ref, nk_hbm, nv_hbm,
    q_scr, k_scr, v_scr, sc, o_scr, group, osem, gsem,
):
    rows, heads, span, _ = kbuf.shape
    requests = len_ref.shape[0]
    first = lax.axis_index("gx") * rows
    whole = []
    for i, (buf, hbm) in enumerate(((kbuf, nk_hbm), (vbuf, nv_hbm))):
        for s in range(rows):
            copy = pltpu.make_async_copy(buf.at[s], hbm.at[s], osem.at[2 * s + i])
            copy.start()
            whole.append((s, i, copy))
    lane = lax.broadcasted_iota(jnp.int32, (1, HD), 1)
    half = ROT // 2
    places = lax.broadcasted_iota(jnp.int32, (heads, span), 1)
    bases = []
    for s in range(rows):
        def find(r, value):
            return jnp.where(asg_ref[r] == first + s, len_ref[r], value)
        length = lax.fori_loop(0, requests, find, jnp.int32(1))
        position = length - 1
        angle = position.astype(F32) * freq_ref[...]
        cosine, sine = jnp.cos(angle), jnp.sin(angle)
        c = jnp.where(lane < ROT, cosine, 1.0)
        s1 = jnp.where(lane < half, -sine, 0.0)
        s2 = jnp.where((lane >= half) & (lane < ROT), sine, 0.0)

        def turn(t):
            return t * c + pltpu.roll(t, HD - half, 1) * s1 + pltpu.roll(t, half, 1) * s2

        for h in range(heads):
            for i, scr in enumerate((q_scr, k_scr, v_scr)):
                j = 3 * h + i
                at = j * rows + s
                scr[h : h + 1, :] = qkv_ref[at : at + 1, :] + bq_ref[j : j + 1, :]
        query = turn(q_scr[0:heads, :]).astype(BF16)
        new_key = turn(k_scr[0:heads, :]).astype(BF16).astype(F32)
        new_value = v_scr[0:heads, :].astype(BF16).astype(F32)
        base = pl.multiple_of((position // 16) * 16, 16)
        bases.append(base)
        hit = lax.broadcasted_iota(jnp.int32, (16, HD), 0) == position - base
        for i, (buf, fresh) in enumerate(((kbuf, new_key), (vbuf, new_value))):
            for h in range(heads):
                old = buf[s, h, pl.ds(base, 16), :].astype(F32)
                group[i, s, h] = jnp.where(hit, fresh[h : h + 1, :], old).astype(BF16)
        for h in range(heads):
            sc[h : h + 1, :] = lax.dot_general(
                query[h : h + 1, :], kbuf[s, h], (((1,), (1,)), ((), ())),
                preferred_element_type=F32,
            )
        scale = np.float32(HD**-0.5)
        fresh_score = jnp.sum(query.astype(F32) * new_key, axis=1, keepdims=True) * scale
        scores = jnp.where(places < position, sc[0:heads, :] * scale, -1e30)
        top = jnp.maximum(jnp.max(scores, axis=1, keepdims=True), fresh_score)
        weights = jnp.where(places < position, jnp.exp(scores - top), 0.0)
        fresh_weight = jnp.exp(fresh_score - top)
        total = jnp.sum(weights, axis=1, keepdims=True) + fresh_weight
        low = weights.astype(BF16)
        for h in range(heads):
            o_scr[h : h + 1, :] = jnp.dot(low[h : h + 1, :], vbuf[s, h], preferred_element_type=F32)
        summed = o_scr[0:heads, :] + fresh_weight.astype(BF16).astype(F32) * new_value
        out = (summed / total).astype(BF16).astype(F32)
        for h in range(heads):
            att_ref[s : s + 1, h * HD : (h + 1) * HD] = out[h : h + 1, :]
    parts = []
    for s, i, copy in whole:
        copy.wait()
        part = pltpu.make_async_copy(
            group.at[i, s],
            (nk_hbm, nv_hbm)[i].at[s, :, pl.ds(bases[s], 16), :],
            gsem.at[2 * s + i],
        )
        part.start()
        parts.append(part)
    for part in parts:
        part.wait()


def output_kernel(
    n, m, ny, att_ref, hid_ref, h_ref, asg_ref, bo_ref, bd_ref, wo, wd,
    out_ref,
    h_all, a_all, a_rows, y_send, y_in,
    h_ssem, h_rsem, a_ssem, a_rsem, y_ssem, y_rsem,
):
    me, my = lax.axis_index("gx"), lax.axis_index("gy")
    rows = att_ref.shape[0]
    cols = hid_ref.shape[1]
    barrier = pltpu.get_barrier_semaphore()
    for k in range(1, n):
        pl.semaphore_signal(barrier, inc=1, device_id={"gx": lax.rem(me + k, n)}, device_id_type=MESH)
    for k in range(1, ny):
        pl.semaphore_signal(barrier, inc=1, device_id={"gy": lax.rem(my + k, ny)}, device_id_type=MESH)
    h_all[me] = hid_ref[...]
    a_all[me] = att_ref[...]
    pl.semaphore_wait(barrier, n + ny - 2)
    a_copies, h_copies = [], []
    for k in range(1, n):
        peer = {"gx": lax.rem(me + k, n)}
        h_copies.append(send(h_all.at[me], h_all.at[me], h_ssem.at[k], h_rsem.at[k], peer))
    for k in range(1, n):
        peer = {"gx": lax.rem(me + k, n)}
        a_copies.append(send(a_all.at[me], a_all.at[me], a_ssem.at[k], a_rsem.at[k], peer))
    place = slot_rows(asg_ref)
    x = jnp.dot(place, h_ref[...], preferred_element_type=F32) + (bo_ref[...] + bd_ref[...]).reshape(1, h_ref.shape[1])
    for copy in h_copies:
        copy.wait_recv()
    acc = jnp.zeros(y_send.shape, F32)
    for c in range(m):
        parts = [h_all[g * m + c] for g in range(n // m)]
        block = parts[0] if len(parts) == 1 else jnp.concatenate(parts, axis=0)
        acc = acc + jnp.dot(block, wd[c * cols : (c + 1) * cols, :], preferred_element_type=F32)
    for copy in a_copies:
        copy.wait_recv()
    for p in range(n):
        a_rows[p * rows : (p + 1) * rows, :] = a_all[p]
    acc = acc + jnp.dot(a_rows[...].astype(BF16), wo[...], preferred_element_type=F32)
    y_send[...] = acc.astype(BF16)
    y_copies = []
    for k in range(1, ny):
        peer = {"gy": lax.rem(my + k, ny)}
        y_copies.append(send(y_send, y_in.at[k], y_ssem.at[k], y_rsem.at[k], peer))
    acc = acc + x
    for k in range(1, ny):
        y_copies[k - 1].wait_recv()
        acc = acc + y_in[k].astype(F32)
    out_ref[...] = lax.dot_general(
        place, acc.astype(BF16), (((0,), (0,)), ((), ())), preferred_element_type=F32
    ).astype(BF16)
    for copy in h_copies + a_copies + y_copies:
        copy.wait_send()


def on_device(
    n, ny, hidden_in, norm1_gain, norm1_bias, norm2_gain, norm2_bias, w_qkv, b_qkv, w_out, b_out,
    w_up, b_up, w_down, b_down, key_cache, value_cache, lengths, assignment,
):
    requests, depth = hidden_in.shape
    rows, heads, span, _ = key_cache.shape
    q_cols = w_qkv.shape[1]
    units = w_up.shape[1]
    m = max(c for c in range(1, n + 1) if n % c == 0 and units % c == 0 and (units // c) % 128 == 0)
    u_rows, u_cols = requests // (n // m), units // m
    asg = assignment.reshape(1, requests)
    dma = pltpu.SemaphoreType.DMA
    q_rows = -(-(q_cols // HD * rows) // 16) * 16

    qkv, hid = pl.pallas_call(
        functools.partial(project_kernel, n, m),
        out_shape=(
            jax.ShapeDtypeStruct((q_rows, HD), F32),
            jax.ShapeDtypeStruct((u_rows, u_cols), BF16),
        ),
        in_specs=[VMEM] * 7 + [HBM] * 2,
        out_specs=(VMEM, VMEM),
        scratch_shapes=[
            pltpu.VMEM((depth, q_cols), BF16),
            pltpu.VMEM((m, depth, u_cols), BF16),
            pltpu.VMEM((requests, 128), F32),
            pltpu.VMEM((n, requests, 128), F32),
            pltpu.VMEM((n, q_rows, HD), F32),
            pltpu.VMEM((n, q_rows, HD), BF16),
            pltpu.VMEM((n, q_rows, HD), BF16),
            pltpu.VMEM((requests, u_cols), F32),
            pltpu.VMEM((n, u_rows, u_cols), BF16),
            pltpu.VMEM((n, u_rows, u_cols), BF16),
            dma((m + 1,)),
            dma((n,)), dma((n,)), dma((n,)), dma((n,)), dma((n,)), dma((n,)),
        ],
        compiler_params=pltpu.CompilerParams(
            collective_id=0, has_side_effects=True, vmem_limit_bytes=52 << 20
        ),
        name="project",
    )(
        hidden_in, norm1_gain, norm1_bias, norm2_gain, norm2_bias, asg,
        b_up.reshape(m, 1, u_cols), w_qkv, w_up,
    )

    freq = np.zeros((1, HD), np.float32)
    freq[0, :ROT] = np.tile(10000.0 ** (-2.0 * np.arange(ROT // 2) / ROT), 2)
    padded = -(-heads // 8) * 8
    att, new_keys, new_values = pl.pallas_call(
        attend_kernel,
        out_shape=(
            jax.ShapeDtypeStruct((rows, heads * HD), F32),
            jax.ShapeDtypeStruct(key_cache.shape, BF16),
            jax.ShapeDtypeStruct(value_cache.shape, BF16),
        ),
        in_specs=[SMEM, SMEM, VMEM, VMEM, VMEM, VMEM, VMEM],
        out_specs=(VMEM, ANY, ANY),
        scratch_shapes=[
            pltpu.VMEM((padded, HD), F32),
            pltpu.VMEM((padded, HD), F32),
            pltpu.VMEM((padded, HD), F32),
            pltpu.VMEM((padded, span), F32),
            pltpu.VMEM((padded, HD), F32),
            pltpu.VMEM((2, rows, heads, 16, HD), BF16),
            dma((2 * rows,)),
            dma((2 * rows,)),
        ],
        compiler_params=pltpu.CompilerParams(vmem_limit_bytes=20 << 20),
        name="attend",
    )(lengths, assignment, qkv, b_qkv.reshape(q_cols // HD, HD), jnp.asarray(freq), key_cache, value_cache)

    hidden_out = pl.pallas_call(
        functools.partial(output_kernel, n, m, ny),
        out_shape=jax.ShapeDtypeStruct((requests, depth), BF16),
        in_specs=[VMEM] * 8,
        out_specs=VMEM,
        scratch_shapes=[
            pltpu.VMEM((n, u_rows, u_cols), BF16),
            pltpu.VMEM((n, rows, heads * HD), F32),
            pltpu.VMEM((requests, heads * HD), F32),
            pltpu.VMEM((requests, depth), BF16),
            pltpu.VMEM((ny, requests, depth), BF16),
            dma((n,)), dma((n,)), dma((n,)), dma((n,)), dma((ny,)), dma((ny,)),
        ],
        compiler_params=pltpu.CompilerParams(
            collective_id=1, has_side_effects=True, vmem_limit_bytes=20 << 20
        ),
        name="output",
    )(att, hid, hidden_in, asg, b_out, b_down, w_out, w_down)
    return (hidden_out, new_keys, new_values)


def solution(mesh):
    return jax.shard_map(
        functools.partial(on_device, mesh.shape["gx"], mesh.shape["gy"]),
        mesh=mesh,
        in_specs=(
            P(None, "gx"), P("gx"), P("gx"), P("gx"), P("gx"),
            P("gx", "gy"), P("gy"), P("gy", "gx"), P("gx"),
            P("gx", "gy"), P("gy"), P("gy", "gx"), P("gx"),
            P("gx", "gy", None, None), P("gx", "gy", None, None), P(), P(),
        ),
        out_specs=(P(None, "gx"), P("gx", "gy", None, None), P("gx", "gy", None, None)),
        check_vma=False,
    )
```

```python
import functools

import jax
import jax.numpy as jnp
import numpy as np
from jax import lax
from jax.experimental import pallas as pl
from jax.experimental.pallas import tpu as pltpu
from jax.sharding import PartitionSpec as P

HD = 128
ROT = 32
F32 = jnp.float32
BF16 = jnp.bfloat16
MESH = pl.DeviceIdType.MESH
ANY = pl.BlockSpec(memory_space=pl.ANY)
VMEM = pl.BlockSpec(memory_space=pltpu.VMEM)
SMEM = pl.BlockSpec(memory_space=pltpu.SMEM)
HBM = pl.BlockSpec(memory_space=pltpu.HBM)


def slot_rows(asg_ref):
    requests = asg_ref.shape[1]
    slots = lax.broadcasted_iota(jnp.int32, (requests, requests), 0)
    return jnp.where(slots == asg_ref[...], 1.0, 0.0).astype(BF16)


def send(src, dst, ssem, rsem, where):
    copy = pltpu.make_async_remote_copy(
        src_ref=src, dst_ref=dst, send_sem=ssem, recv_sem=rsem,
        device_id=where, device_id_type=MESH,
    )
    copy.start()
    return copy


def project_kernel(
    n, m, h_hbm, g1_hbm, b1_hbm, g2_hbm, b2_hbm, asg_hbm, bu_hbm, wq_hbm, wu_hbm,
    qkv_ref, hid_ref,
    h_ref, g1_ref, b1_ref, g2_ref, b2_ref, asg_ref, bu_ref, small_sem,
    wq, wu, st_own, st_in, q_wide, q_send, q_in, u_part, u_send, u_in,
    wsem, s_ssem, s_rsem, q_ssem, q_rsem, u_ssem, u_rsem,
):
    me = lax.axis_index("gx")
    rg_count = n // m
    requests, depth = h_ref.shape
    rows = requests // n
    tiles = wq.shape[1] // HD
    u_rows, u_cols = u_send.shape[1:]
    my_col, my_group = lax.rem(me, m), me // m
    pairs = (
        (asg_hbm, asg_ref), (h_hbm, h_ref), (g1_hbm, g1_ref), (b1_hbm, b1_ref),
        (g2_hbm, g2_ref), (b2_hbm, b2_ref), (bu_hbm, bu_ref),
    )
    small = [pltpu.make_async_copy(a, b, small_sem.at[i]) for i, (a, b) in enumerate(pairs)]
    for copy in small:
        copy.start()
    load_q = pltpu.make_async_copy(wq_hbm, wq, wsem.at[m])
    load_q.start()
    order = list(range(1, m)) + [0]
    loads = {}
    for k in order:
        col = lax.rem(my_col + k, m)
        loads[k] = pltpu.make_async_copy(
            wu_hbm.at[:, pl.ds(pl.multiple_of(col * u_cols, 128), u_cols)], wu.at[k], wsem.at[k]
        )
        loads[k].start()
    barrier = pltpu.get_barrier_semaphore()
    for k in range(1, n):
        pl.semaphore_signal(barrier, inc=1, device_id={"gx": lax.rem(me + k, n)}, device_id_type=MESH)

    for copy in small:
        copy.wait()
    place = slot_rows(asg_ref)
    x = jnp.dot(place, h_ref[...], preferred_element_type=F32)
    sums = jnp.sum(x, axis=1, keepdims=True)
    squares = jnp.sum(x * x, axis=1, keepdims=True)
    lane = lax.broadcasted_iota(jnp.int32, (requests, 128), 1)
    st_own[...] = jnp.where(lane == 0, sums, jnp.where(lane == 1, squares, 0.0))
    pl.semaphore_wait(barrier, n - 1)
    stats = [
        send(st_own, st_in.at[k], s_ssem.at[k], s_rsem.at[k], {"gx": lax.rem(me + k, n)})
        for k in range(1, n)
    ]
    total = st_own[...]
    for k in range(1, n):
        stats[k - 1].wait_recv()
        total = total + st_in[k]
    width = depth * n
    mean = total[:, 0:1] / width
    var = total[:, 1:2] / width - mean * mean
    normed = (x - mean) * lax.rsqrt(var + 1e-05)
    attn_in = (normed * g1_ref[...].reshape(1, depth) + b1_ref[...].reshape(1, depth)).astype(BF16)
    mlp_in = (normed * g2_ref[...].reshape(1, depth) + b2_ref[...].reshape(1, depth)).astype(BF16)

    load_q.wait()
    qkv = jnp.dot(attn_in, wq[...], preferred_element_type=F32)
    for p in range(n):
        for j in range(tiles):
            q_wide[p, j * rows : (j + 1) * rows, :] = qkv[
                p * rows : (p + 1) * rows, j * HD : (j + 1) * HD
            ]
    q_send[...] = q_wide[...].astype(BF16)
    q_copies = []
    for k in range(1, n):
        peer = lax.rem(me + k, n)
        q_copies.append(send(q_send.at[peer], q_in.at[k], q_ssem.at[k], q_rsem.at[k], {"gx": peer}))
    u_copies = []
    for k in order:
        loads[k].wait()
        part = jnp.dot(mlp_in, wu[k], preferred_element_type=F32)
        if rg_count > 1:
            u_part[...] = part
        for j in list(range(1, rg_count)) + [0]:
            group = lax.rem(my_group + j, rg_count)
            peer = group * m + lax.rem(my_col + k, m)
            at = j * m + k
            if rg_count > 1:
                own = u_part[pl.ds(pl.multiple_of(group * u_rows, u_rows), u_rows), :]
            else:
                own = part
            u_send[at] = own.astype(BF16)
            if at:
                u_copies.append(send(u_send.at[at], u_in.at[at], u_ssem.at[at], u_rsem.at[at], {"gx": peer}))
    total_q = q_wide[me]
    for k in range(1, n):
        q_copies[k - 1].wait_recv()
        total_q = total_q + q_in[k].astype(F32)
    qkv_ref[...] = total_q
    for copy in u_copies:
        copy.wait_recv()
    up = own.astype(F32) + bu_ref[my_col]
    for at in range(1, n):
        up = up + u_in[at].astype(F32)
    hid_ref[...] = (0.5 * up * (1.0 + lax.erf(up * np.float32(0.5**0.5)))).astype(BF16)
    for copy in stats + q_copies + u_copies:
        copy.wait_send()


def attend_kernel(
    len_ref, asg_ref, qkv_ref, bq_ref, freq_ref, kbuf, vbuf,
    att_ref, nk_hbm, nv_hbm,
    q_scr, k_scr, v_scr, sc, o_scr, group, osem, gsem,
):
    rows, heads, span, _ = kbuf.shape
    requests = len_ref.shape[0]
    first = lax.axis_index("gx") * rows
    whole = []
    for i, (buf, hbm) in enumerate(((kbuf, nk_hbm), (vbuf, nv_hbm))):
        for s in range(rows):
            copy = pltpu.make_async_copy(buf.at[s], hbm.at[s], osem.at[2 * s + i])
            copy.start()
            whole.append((s, i, copy))
    lane = lax.broadcasted_iota(jnp.int32, (1, HD), 1)
    half = ROT // 2
    places = lax.broadcasted_iota(jnp.int32, (heads, span), 1)
    bases = []
    for s in range(rows):
        def find(r, value):
            return jnp.where(asg_ref[r] == first + s, len_ref[r], value)
        length = lax.fori_loop(0, requests, find, jnp.int32(1))
        position = length - 1
        angle = position.astype(F32) * freq_ref[...]
        cosine, sine = jnp.cos(angle), jnp.sin(angle)
        c = jnp.where(lane < ROT, cosine, 1.0)
        s1 = jnp.where(lane < half, -sine, 0.0)
        s2 = jnp.where((lane >= half) & (lane < ROT), sine, 0.0)

        def turn(t):
            return t * c + pltpu.roll(t, HD - half, 1) * s1 + pltpu.roll(t, half, 1) * s2

        for h in range(heads):
            for i, scr in enumerate((q_scr, k_scr, v_scr)):
                j = 3 * h + i
                at = j * rows + s
                scr[h : h + 1, :] = qkv_ref[at : at + 1, :] + bq_ref[j : j + 1, :]
        query = turn(q_scr[0:heads, :]).astype(BF16)
        new_key = turn(k_scr[0:heads, :]).astype(BF16).astype(F32)
        new_value = v_scr[0:heads, :].astype(BF16).astype(F32)
        base = pl.multiple_of((position // 16) * 16, 16)
        bases.append(base)
        hit = lax.broadcasted_iota(jnp.int32, (16, HD), 0) == position - base
        for i, (buf, fresh) in enumerate(((kbuf, new_key), (vbuf, new_value))):
            for h in range(heads):
                old = buf[s, h, pl.ds(base, 16), :].astype(F32)
                group[i, s, h] = jnp.where(hit, fresh[h : h + 1, :], old).astype(BF16)
        for h in range(heads):
            sc[h : h + 1, :] = lax.dot_general(
                query[h : h + 1, :], kbuf[s, h], (((1,), (1,)), ((), ())),
                preferred_element_type=F32,
            )
        scale = np.float32(HD**-0.5)
        fresh_score = jnp.sum(query.astype(F32) * new_key, axis=1, keepdims=True) * scale
        scores = jnp.where(places < position, sc[0:heads, :] * scale, -1e30)
        top = jnp.maximum(jnp.max(scores, axis=1, keepdims=True), fresh_score)
        weights = jnp.where(places < position, jnp.exp(scores - top), 0.0)
        fresh_weight = jnp.exp(fresh_score - top)
        total = jnp.sum(weights, axis=1, keepdims=True) + fresh_weight
        low = weights.astype(BF16)
        for h in range(heads):
            o_scr[h : h + 1, :] = jnp.dot(low[h : h + 1, :], vbuf[s, h], preferred_element_type=F32)
        summed = o_scr[0:heads, :] + fresh_weight.astype(BF16).astype(F32) * new_value
        out = (summed / total).astype(BF16).astype(F32)
        for h in range(heads):
            att_ref[s : s + 1, h * HD : (h + 1) * HD] = out[h : h + 1, :]
    parts = []
    for s, i, copy in whole:
        copy.wait()
        part = pltpu.make_async_copy(
            group.at[i, s],
            (nk_hbm, nv_hbm)[i].at[s, :, pl.ds(bases[s], 16), :],
            gsem.at[2 * s + i],
        )
        part.start()
        parts.append(part)
    for part in parts:
        part.wait()


def output_kernel(
    n, m, ny, att_ref, hid_ref, h_ref, asg_ref, bo_ref, bd_ref, wo, wd,
    out_ref,
    h_all, a_all, a_rows, y_send, y_in,
    h_ssem, h_rsem, a_ssem, a_rsem, y_ssem, y_rsem,
):
    me, my = lax.axis_index("gx"), lax.axis_index("gy")
    rows = att_ref.shape[0]
    cols = hid_ref.shape[1]
    barrier = pltpu.get_barrier_semaphore()
    for k in range(1, n):
        pl.semaphore_signal(barrier, inc=1, device_id={"gx": lax.rem(me + k, n)}, device_id_type=MESH)
    for k in range(1, ny):
        pl.semaphore_signal(barrier, inc=1, device_id={"gy": lax.rem(my + k, ny)}, device_id_type=MESH)
    h_all[me] = hid_ref[...]
    a_all[me] = att_ref[...]
    pl.semaphore_wait(barrier, n + ny - 2)
    a_copies, h_copies = [], []
    for k in range(1, n):
        peer = {"gx": lax.rem(me + k, n)}
        h_copies.append(send(h_all.at[me], h_all.at[me], h_ssem.at[k], h_rsem.at[k], peer))
    for k in range(1, n):
        peer = {"gx": lax.rem(me + k, n)}
        a_copies.append(send(a_all.at[me], a_all.at[me], a_ssem.at[k], a_rsem.at[k], peer))
    place = slot_rows(asg_ref)
    x = jnp.dot(place, h_ref[...], preferred_element_type=F32) + (bo_ref[...] + bd_ref[...]).reshape(1, h_ref.shape[1])
    for copy in h_copies:
        copy.wait_recv()
    acc = jnp.zeros(y_send.shape, F32)
    for c in range(m):
        parts = [h_all[g * m + c] for g in range(n // m)]
        block = parts[0] if len(parts) == 1 else jnp.concatenate(parts, axis=0)
        acc = acc + jnp.dot(block, wd[c * cols : (c + 1) * cols, :], preferred_element_type=F32)
    for copy in a_copies:
        copy.wait_recv()
    for p in range(n):
        a_rows[p * rows : (p + 1) * rows, :] = a_all[p]
    acc = acc + jnp.dot(a_rows[...].astype(BF16), wo[...], preferred_element_type=F32)
    y_send[...] = acc.astype(BF16)
    y_copies = []
    for k in range(1, ny):
        peer = {"gy": lax.rem(my + k, ny)}
        y_copies.append(send(y_send, y_in.at[k], y_ssem.at[k], y_rsem.at[k], peer))
    acc = acc + x
    for k in range(1, ny):
        y_copies[k - 1].wait_recv()
        acc = acc + y_in[k].astype(F32)
    out_ref[...] = lax.dot_general(
        place, acc.astype(BF16), (((0,), (0,)), ((), ())), preferred_element_type=F32
    ).astype(BF16)
    for copy in h_copies + a_copies + y_copies:
        copy.wait_send()


def on_device(
    n, ny, hidden_in, norm1_gain, norm1_bias, norm2_gain, norm2_bias, w_qkv, b_qkv, w_out, b_out,
    w_up, b_up, w_down, b_down, key_cache, value_cache, lengths, assignment,
):
    requests, depth = hidden_in.shape
    rows, heads, span, _ = key_cache.shape
    q_cols = w_qkv.shape[1]
    units = w_up.shape[1]
    m = max(c for c in range(1, n + 1) if n % c == 0 and units % c == 0 and (units // c) % 128 == 0)
    u_rows, u_cols = requests // (n // m), units // m
    asg = assignment.reshape(1, requests)
    dma = pltpu.SemaphoreType.DMA
    q_rows = -(-(q_cols // HD * rows) // 16) * 16

    qkv, hid = pl.pallas_call(
        functools.partial(project_kernel, n, m),
        out_shape=(
            jax.ShapeDtypeStruct((q_rows, HD), F32),
            jax.ShapeDtypeStruct((u_rows, u_cols), BF16),
        ),
        in_specs=[HBM] * 9,
        out_specs=(VMEM, VMEM),
        scratch_shapes=[
            pltpu.VMEM((requests, depth), BF16),
            pltpu.VMEM((depth,), F32),
            pltpu.VMEM((depth,), F32),
            pltpu.VMEM((depth,), F32),
            pltpu.VMEM((depth,), F32),
            pltpu.VMEM((1, requests), jnp.int32),
            pltpu.VMEM((m, 1, u_cols), F32),
            dma((7,)),
            pltpu.VMEM((depth, q_cols), BF16),
            pltpu.VMEM((m, depth, u_cols), BF16),
            pltpu.VMEM((requests, 128), F32),
            pltpu.VMEM((n, requests, 128), F32),
            pltpu.VMEM((n, q_rows, HD), F32),
            pltpu.VMEM((n, q_rows, HD), BF16),
            pltpu.VMEM((n, q_rows, HD), BF16),
            pltpu.VMEM((requests, u_cols), F32),
            pltpu.VMEM((n, u_rows, u_cols), BF16),
            pltpu.VMEM((n, u_rows, u_cols), BF16),
            dma((m + 1,)),
            dma((n,)), dma((n,)), dma((n,)), dma((n,)), dma((n,)), dma((n,)),
        ],
        compiler_params=pltpu.CompilerParams(
            collective_id=0, has_side_effects=True, vmem_limit_bytes=(54 << 20) - (60 << 10)
        ),
        name="project",
    )(
        hidden_in, norm1_gain, norm1_bias, norm2_gain, norm2_bias, asg,
        b_up.reshape(m, 1, u_cols), w_qkv, w_up,
    )

    freq = np.zeros((1, HD), np.float32)
    freq[0, :ROT] = np.tile(10000.0 ** (-2.0 * np.arange(ROT // 2) / ROT), 2)
    padded = -(-heads // 8) * 8
    att, new_keys, new_values = pl.pallas_call(
        attend_kernel,
        out_shape=(
            jax.ShapeDtypeStruct((rows, heads * HD), F32),
            jax.ShapeDtypeStruct(key_cache.shape, BF16),
            jax.ShapeDtypeStruct(value_cache.shape, BF16),
        ),
        in_specs=[SMEM, SMEM, VMEM, VMEM, VMEM, VMEM, VMEM],
        out_specs=(VMEM, ANY, ANY),
        scratch_shapes=[
            pltpu.VMEM((padded, HD), F32),
            pltpu.VMEM((padded, HD), F32),
            pltpu.VMEM((padded, HD), F32),
            pltpu.VMEM((padded, span), F32),
            pltpu.VMEM((padded, HD), F32),
            pltpu.VMEM((2, rows, heads, 16, HD), BF16),
            dma((2 * rows,)),
            dma((2 * rows,)),
        ],
        compiler_params=pltpu.CompilerParams(vmem_limit_bytes=20 << 20),
        name="attend",
    )(lengths, assignment, qkv, b_qkv.reshape(q_cols // HD, HD), jnp.asarray(freq), key_cache, value_cache)

    hidden_out = pl.pallas_call(
        functools.partial(output_kernel, n, m, ny),
        out_shape=jax.ShapeDtypeStruct((requests, depth), BF16),
        in_specs=[VMEM] * 8,
        out_specs=VMEM,
        scratch_shapes=[
            pltpu.VMEM((n, u_rows, u_cols), BF16),
            pltpu.VMEM((n, rows, heads * HD), F32),
            pltpu.VMEM((requests, heads * HD), F32),
            pltpu.VMEM((requests, depth), BF16),
            pltpu.VMEM((ny, requests, depth), BF16),
            dma((n,)), dma((n,)), dma((n,)), dma((n,)), dma((ny,)), dma((ny,)),
        ],
        compiler_params=pltpu.CompilerParams(
            collective_id=1, has_side_effects=True, vmem_limit_bytes=20 << 20
        ),
        name="output",
    )(att, hid, hidden_in, asg, b_out, b_down, w_out, w_down)
    return (hidden_out, new_keys, new_values)


def solution(mesh):
    return jax.shard_map(
        functools.partial(on_device, mesh.shape["gx"], mesh.shape["gy"]),
        mesh=mesh,
        in_specs=(
            P(None, "gx"), P("gx"), P("gx"), P("gx"), P("gx"),
            P("gx", "gy"), P("gy"), P("gy", "gx"), P("gx"),
            P("gx", "gy"), P("gy"), P("gy", "gx"), P("gx"),
            P("gx", "gy", None, None), P("gx", "gy", None, None), P(), P(),
        ),
        out_specs=(P(None, "gx"), P("gx", "gy", None, None), P("gx", "gy", None, None)),
        check_vma=False,
    )
```

```python
import functools

import jax
import jax.numpy as jnp
import numpy as np
from jax import lax
from jax.experimental import pallas as pl
from jax.experimental.pallas import tpu as pltpu
from jax.sharding import PartitionSpec as P

HD = 128
ROT = 32
F32 = jnp.float32
BF16 = jnp.bfloat16
MESH = pl.DeviceIdType.MESH
ANY = pl.BlockSpec(memory_space=pl.ANY)
VMEM = pl.BlockSpec(memory_space=pltpu.VMEM)
SMEM = pl.BlockSpec(memory_space=pltpu.SMEM)
HBM = pl.BlockSpec(memory_space=pltpu.HBM)


def slot_rows(asg_ref):
    requests = asg_ref.shape[1]
    slots = lax.broadcasted_iota(jnp.int32, (requests, requests), 0)
    return jnp.where(slots == asg_ref[...], 1.0, 0.0).astype(BF16)


def send(src, dst, ssem, rsem, where):
    copy = pltpu.make_async_remote_copy(
        src_ref=src, dst_ref=dst, send_sem=ssem, recv_sem=rsem,
        device_id=where, device_id_type=MESH,
    )
    copy.start()
    return copy


def project_kernel(
    n, m, h_ref, vec_ref, asg_ref, bu_ref, wq_hbm, wu_hbm,
    qkv_ref, hid_ref,
    wq, wu, st_own, st_in, q_wide, q_send, q_in, u_part, u_send, u_in,
    wsem, s_ssem, s_rsem, q_ssem, q_rsem, u_ssem, u_rsem,
):
    me = lax.axis_index("gx")
    rg_count = n // m
    requests, depth = h_ref.shape
    rows = requests // n
    tiles = wq.shape[1] // HD
    u_rows, u_cols = u_send.shape[1:]
    my_col, my_group = lax.rem(me, m), me // m
    load_q = pltpu.make_async_copy(wq_hbm, wq, wsem.at[m])
    load_q.start()
    order = list(range(1, m)) + [0]
    loads = {}
    for k in order:
        col = lax.rem(my_col + k, m)
        loads[k] = pltpu.make_async_copy(
            wu_hbm.at[:, pl.ds(pl.multiple_of(col * u_cols, 128), u_cols)], wu.at[k], wsem.at[k]
        )
        loads[k].start()
    barrier = pltpu.get_barrier_semaphore()
    for k in range(1, n):
        pl.semaphore_signal(barrier, inc=1, device_id={"gx": lax.rem(me + k, n)}, device_id_type=MESH)

    place = slot_rows(asg_ref)
    x = jnp.dot(place, h_ref[...], preferred_element_type=F32)
    sums = jnp.sum(x, axis=1, keepdims=True)
    squares = jnp.sum(x * x, axis=1, keepdims=True)
    lane = lax.broadcasted_iota(jnp.int32, (requests, 128), 1)
    st_own[...] = jnp.where(lane == 0, sums, jnp.where(lane == 1, squares, 0.0))
    pl.semaphore_wait(barrier, n - 1)
    stats = [
        send(st_own, st_in.at[k], s_ssem.at[k], s_rsem.at[k], {"gx": lax.rem(me + k, n)})
        for k in range(1, n)
    ]
    total = st_own[...]
    for k in range(1, n):
        stats[k - 1].wait_recv()
        total = total + st_in[k]
    width = depth * n
    mean = total[:, 0:1] / width
    var = total[:, 1:2] / width - mean * mean
    normed = (x - mean) * lax.rsqrt(var + 1e-05)
    attn_in = (normed * vec_ref[0:1, :] + vec_ref[1:2, :]).astype(BF16)
    mlp_in = (normed * vec_ref[2:3, :] + vec_ref[3:4, :]).astype(BF16)

    load_q.wait()
    qkv = jnp.dot(attn_in, wq[...], preferred_element_type=F32)
    for p in range(n):
        for j in range(tiles):
            q_wide[p, j * rows : (j + 1) * rows, :] = qkv[
                p * rows : (p + 1) * rows, j * HD : (j + 1) * HD
            ]
    q_send[...] = q_wide[...].astype(BF16)
    q_copies = []
    for k in range(1, n):
        peer = lax.rem(me + k, n)
        q_copies.append(send(q_send.at[peer], q_in.at[k], q_ssem.at[k], q_rsem.at[k], {"gx": peer}))
    u_copies = []
    for k in order:
        loads[k].wait()
        part = jnp.dot(mlp_in, wu[k], preferred_element_type=F32)
        if rg_count > 1:
            u_part[...] = part
        for j in list(range(1, rg_count)) + [0]:
            group = lax.rem(my_group + j, rg_count)
            peer = group * m + lax.rem(my_col + k, m)
            at = j * m + k
            if rg_count > 1:
                own = u_part[pl.ds(pl.multiple_of(group * u_rows, u_rows), u_rows), :]
            else:
                own = part
            u_send[at] = own.astype(BF16)
            if at:
                u_copies.append(send(u_send.at[at], u_in.at[at], u_ssem.at[at], u_rsem.at[at], {"gx": peer}))
    total_q = q_wide[me]
    for k in range(1, n):
        q_copies[k - 1].wait_recv()
        total_q = total_q + q_in[k].astype(F32)
    qkv_ref[...] = total_q
    for copy in u_copies:
        copy.wait_recv()
    up = own.astype(F32) + bu_ref[my_col]
    for at in range(1, n):
        up = up + u_in[at].astype(F32)
    hid_ref[...] = (0.5 * up * (1.0 + lax.erf(up * np.float32(0.5**0.5)))).astype(BF16)
    for copy in stats + q_copies + u_copies:
        copy.wait_send()


def attend_kernel(
    len_ref, asg_ref, qkv_ref, bq_ref, freq_ref, kbuf, vbuf,
    att_ref, nk_hbm, nv_hbm,
    q_scr, k_scr, v_scr, sc, o_scr, group, osem, gsem,
):
    rows, heads, span, _ = kbuf.shape
    requests = len_ref.shape[0]
    first = lax.axis_index("gx") * rows
    whole = []
    for i, (buf, hbm) in enumerate(((kbuf, nk_hbm), (vbuf, nv_hbm))):
        for s in range(rows):
            copy = pltpu.make_async_copy(buf.at[s], hbm.at[s], osem.at[2 * s + i])
            copy.start()
            whole.append((s, i, copy))
    lane = lax.broadcasted_iota(jnp.int32, (1, HD), 1)
    half = ROT // 2
    places = lax.broadcasted_iota(jnp.int32, (heads, span), 1)
    bases = []
    for s in range(rows):
        def find(r, value):
            return jnp.where(asg_ref[r] == first + s, len_ref[r], value)
        length = lax.fori_loop(0, requests, find, jnp.int32(1))
        position = length - 1
        angle = position.astype(F32) * freq_ref[...]
        cosine, sine = jnp.cos(angle), jnp.sin(angle)
        c = jnp.where(lane < ROT, cosine, 1.0)
        s1 = jnp.where(lane < half, -sine, 0.0)
        s2 = jnp.where((lane >= half) & (lane < ROT), sine, 0.0)

        def turn(t):
            return t * c + pltpu.roll(t, HD - half, 1) * s1 + pltpu.roll(t, half, 1) * s2

        for h in range(heads):
            for i, scr in enumerate((q_scr, k_scr, v_scr)):
                j = 3 * h + i
                at = j * rows + s
                scr[h : h + 1, :] = qkv_ref[at : at + 1, :] + bq_ref[j : j + 1, :]
        query = turn(q_scr[0:heads, :]).astype(BF16)
        new_key = turn(k_scr[0:heads, :]).astype(BF16).astype(F32)
        new_value = v_scr[0:heads, :].astype(BF16).astype(F32)
        base = pl.multiple_of((position // 16) * 16, 16)
        bases.append(base)
        hit = lax.broadcasted_iota(jnp.int32, (16, HD), 0) == position - base
        for i, (buf, fresh) in enumerate(((kbuf, new_key), (vbuf, new_value))):
            for h in range(heads):
                old = buf[s, h, pl.ds(base, 16), :].astype(F32)
                group[i, s, h] = jnp.where(hit, fresh[h : h + 1, :], old).astype(BF16)
        for h in range(heads):
            sc[h : h + 1, :] = lax.dot_general(
                query[h : h + 1, :], kbuf[s, h], (((1,), (1,)), ((), ())),
                preferred_element_type=F32,
            )
        scale = np.float32(HD**-0.5)
        fresh_score = jnp.sum(query.astype(F32) * new_key, axis=1, keepdims=True) * scale
        scores = jnp.where(places < position, sc[0:heads, :] * scale, -1e30)
        top = jnp.maximum(jnp.max(scores, axis=1, keepdims=True), fresh_score)
        weights = jnp.where(places < position, jnp.exp(scores - top), 0.0)
        fresh_weight = jnp.exp(fresh_score - top)
        total = jnp.sum(weights, axis=1, keepdims=True) + fresh_weight
        low = weights.astype(BF16)
        for h in range(heads):
            o_scr[h : h + 1, :] = jnp.dot(low[h : h + 1, :], vbuf[s, h], preferred_element_type=F32)
        summed = o_scr[0:heads, :] + fresh_weight.astype(BF16).astype(F32) * new_value
        out = (summed / total).astype(BF16).astype(F32)
        for h in range(heads):
            att_ref[s : s + 1, h * HD : (h + 1) * HD] = out[h : h + 1, :]
    parts = []
    for s, i, copy in whole:
        copy.wait()
        part = pltpu.make_async_copy(
            group.at[i, s],
            (nk_hbm, nv_hbm)[i].at[s, :, pl.ds(bases[s], 16), :],
            gsem.at[2 * s + i],
        )
        part.start()
        parts.append(part)
    for part in parts:
        part.wait()


def output_kernel(
    n, m, ny, att_ref, hid_ref, h_ref, asg_ref, bo_ref, bd_ref, wo, wd,
    out_ref,
    h_all, a_all, a_rows, y_send, y_in,
    h_ssem, h_rsem, a_ssem, a_rsem, y_ssem, y_rsem,
):
    me, my = lax.axis_index("gx"), lax.axis_index("gy")
    rows = att_ref.shape[0]
    cols = hid_ref.shape[1]
    barrier = pltpu.get_barrier_semaphore()
    for k in range(1, n):
        pl.semaphore_signal(barrier, inc=1, device_id={"gx": lax.rem(me + k, n)}, device_id_type=MESH)
    for k in range(1, ny):
        pl.semaphore_signal(barrier, inc=1, device_id={"gy": lax.rem(my + k, ny)}, device_id_type=MESH)
    h_all[me] = hid_ref[...]
    a_all[me] = att_ref[...]
    pl.semaphore_wait(barrier, n + ny - 2)
    a_copies, h_copies = [], []
    for k in range(1, n):
        peer = {"gx": lax.rem(me + k, n)}
        h_copies.append(send(h_all.at[me], h_all.at[me], h_ssem.at[k], h_rsem.at[k], peer))
    for k in range(1, n):
        peer = {"gx": lax.rem(me + k, n)}
        a_copies.append(send(a_all.at[me], a_all.at[me], a_ssem.at[k], a_rsem.at[k], peer))
    place = slot_rows(asg_ref)
    x = jnp.dot(place, h_ref[...], preferred_element_type=F32) + (bo_ref[...] + bd_ref[...]).reshape(1, h_ref.shape[1])
    for copy in h_copies:
        copy.wait_recv()
    acc = jnp.zeros(y_send.shape, F32)
    for c in range(m):
        parts = [h_all[g * m + c] for g in range(n // m)]
        block = parts[0] if len(parts) == 1 else jnp.concatenate(parts, axis=0)
        acc = acc + jnp.dot(block, wd[c * cols : (c + 1) * cols, :], preferred_element_type=F32)
    for copy in a_copies:
        copy.wait_recv()
    for p in range(n):
        a_rows[p * rows : (p + 1) * rows, :] = a_all[p]
    acc = acc + jnp.dot(a_rows[...].astype(BF16), wo[...], preferred_element_type=F32)
    y_send[...] = acc.astype(BF16)
    y_copies = []
    for k in range(1, ny):
        peer = {"gy": lax.rem(my + k, ny)}
        y_copies.append(send(y_send, y_in.at[k], y_ssem.at[k], y_rsem.at[k], peer))
    acc = acc + x
    for k in range(1, ny):
        y_copies[k - 1].wait_recv()
        acc = acc + y_in[k].astype(F32)
    out_ref[...] = lax.dot_general(
        place, acc.astype(BF16), (((0,), (0,)), ((), ())), preferred_element_type=F32
    ).astype(BF16)
    for copy in h_copies + a_copies + y_copies:
        copy.wait_send()


def on_device(
    n, ny, hidden_in, norm1_gain, norm1_bias, norm2_gain, norm2_bias, w_qkv, b_qkv, w_out, b_out,
    w_up, b_up, w_down, b_down, key_cache, value_cache, lengths, assignment,
):
    requests, depth = hidden_in.shape
    rows, heads, span, _ = key_cache.shape
    q_cols = w_qkv.shape[1]
    units = w_up.shape[1]
    m = max(c for c in range(1, n + 1) if n % c == 0 and units % c == 0 and (units // c) % 128 == 0)
    u_rows, u_cols = requests // (n // m), units // m
    asg = assignment.reshape(1, requests)
    dma = pltpu.SemaphoreType.DMA
    q_rows = -(-(q_cols // HD * rows) // 16) * 16

    qkv, hid = pl.pallas_call(
        functools.partial(project_kernel, n, m),
        out_shape=(
            jax.ShapeDtypeStruct((q_rows, HD), F32),
            jax.ShapeDtypeStruct((u_rows, u_cols), BF16),
        ),
        in_specs=[VMEM] * 4 + [HBM] * 2,
        out_specs=(VMEM, VMEM),
        scratch_shapes=[
            pltpu.VMEM((depth, q_cols), BF16),
            pltpu.VMEM((m, depth, u_cols), BF16),
            pltpu.VMEM((requests, 128), F32),
            pltpu.VMEM((n, requests, 128), F32),
            pltpu.VMEM((n, q_rows, HD), F32),
            pltpu.VMEM((n, q_rows, HD), BF16),
            pltpu.VMEM((n, q_rows, HD), BF16),
            pltpu.VMEM((requests, u_cols), F32),
            pltpu.VMEM((n, u_rows, u_cols), BF16),
            pltpu.VMEM((n, u_rows, u_cols), BF16),
            dma((m + 1,)),
            dma((n,)), dma((n,)), dma((n,)), dma((n,)), dma((n,)), dma((n,)),
        ],
        compiler_params=pltpu.CompilerParams(
            collective_id=0, has_side_effects=True, vmem_limit_bytes=52 << 20
        ),
        name="project",
    )(
        hidden_in, jnp.stack([norm1_gain, norm1_bias, norm2_gain, norm2_bias]), asg,
        b_up.reshape(m, 1, u_cols), w_qkv, w_up,
    )

    freq = np.zeros((1, HD), np.float32)
    freq[0, :ROT] = np.tile(10000.0 ** (-2.0 * np.arange(ROT // 2) / ROT), 2)
    padded = -(-heads // 8) * 8
    att, new_keys, new_values = pl.pallas_call(
        attend_kernel,
        out_shape=(
            jax.ShapeDtypeStruct((rows, heads * HD), F32),
            jax.ShapeDtypeStruct(key_cache.shape, BF16),
            jax.ShapeDtypeStruct(value_cache.shape, BF16),
        ),
        in_specs=[SMEM, SMEM, VMEM, VMEM, VMEM, VMEM, VMEM],
        out_specs=(VMEM, ANY, ANY),
        scratch_shapes=[
            pltpu.VMEM((padded, HD), F32),
            pltpu.VMEM((padded, HD), F32),
            pltpu.VMEM((padded, HD), F32),
            pltpu.VMEM((padded, span), F32),
            pltpu.VMEM((padded, HD), F32),
            pltpu.VMEM((2, rows, heads, 16, HD), BF16),
            dma((2 * rows,)),
            dma((2 * rows,)),
        ],
        compiler_params=pltpu.CompilerParams(vmem_limit_bytes=20 << 20),
        name="attend",
    )(lengths, assignment, qkv, b_qkv.reshape(q_cols // HD, HD), jnp.asarray(freq), key_cache, value_cache)

    hidden_out = pl.pallas_call(
        functools.partial(output_kernel, n, m, ny),
        out_shape=jax.ShapeDtypeStruct((requests, depth), BF16),
        in_specs=[VMEM] * 8,
        out_specs=VMEM,
        scratch_shapes=[
            pltpu.VMEM((n, u_rows, u_cols), BF16),
            pltpu.VMEM((n, rows, heads * HD), F32),
            pltpu.VMEM((requests, heads * HD), F32),
            pltpu.VMEM((requests, depth), BF16),
            pltpu.VMEM((ny, requests, depth), BF16),
            dma((n,)), dma((n,)), dma((n,)), dma((n,)), dma((ny,)), dma((ny,)),
        ],
        compiler_params=pltpu.CompilerParams(
            collective_id=1, has_side_effects=True, vmem_limit_bytes=20 << 20
        ),
        name="output",
    )(att, hid, hidden_in, asg, b_out, b_down, w_out, w_down)
    return (hidden_out, new_keys, new_values)


def solution(mesh):
    return jax.shard_map(
        functools.partial(on_device, mesh.shape["gx"], mesh.shape["gy"]),
        mesh=mesh,
        in_specs=(
            P(None, "gx"), P("gx"), P("gx"), P("gx"), P("gx"),
            P("gx", "gy"), P("gy"), P("gy", "gx"), P("gx"),
            P("gx", "gy"), P("gy"), P("gy", "gx"), P("gx"),
            P("gx", "gy", None, None), P("gx", "gy", None, None), P(), P(),
        ),
        out_specs=(P(None, "gx"), P("gx", "gy", None, None), P("gx", "gy", None, None)),
        check_vma=False,
    )
```
